32 devices in a mesh: region: 4 (over y, core), seq: 8 (over z, x).
Axes of the slice: x: 2, y: 2, z: 4, core: 2. Of those that a mesh axis runs over, the one named last changes fastest.
Arguments:
- scan_tokens: bfloat16 [32768, 1024], P(('region', 'seq')), may hold values from -6 to 6
- grid_tokens: bfloat16 [8192, 1024], P(('region', 'seq')), may hold values from -6 to 6
- seg_slot: int32 [256], P(('region', 'seq')), may hold values from 0 to 255, as said below
- segment_lists: int32 [64, 8], P(('region', 'seq')), may hold values from 0 to 255, as said below
- query_weight: bfloat16 [1024, 1024], replicated, may hold values from -4 to 4
- key_weight: bfloat16 [1024, 1024], replicated, may hold values from -4 to 4
- value_weight: bfloat16 [1024, 1024], replicated, may hold values from -0.1875 to 0.1875
- mixer_weight: bfloat16 [1024, 1024], replicated, may hold values from -0.1875 to 0.1875
- packed_weight: bfloat16 [1024, 3072], replicated, may hold values from -4 to 4
- merged_weight: bfloat16 [1024, 1024], replicated, may hold values from -0.1875 to 0.1875
Outputs:
- encoded: bfloat16 [8192, 1024], P(('region', 'seq'))
The draws below stay inside these ranges and needn't reach their ends.
Inputs may be any that keep to these rules, and one draw needn't show every extreme that they name: `seg_slot`: A permutation: each of the 256 segment slots holds exactly one segment. `segment_lists`: the 8 segments of a query block are held by 8 different devices, all of the block's own region (the devices that share the block's device's index along region); so the blocks of one device name at most 2 segments held by any one device, and in every draw and every region some device holds a segment of every query block of that region.
All inputs are finite; a program needn't handle non-finite values.
Results may differ from the reference program's by a relative error of at most 0.01.
The reference program's roundings to bfloat16 on the way count: a program that leaves them out, or rounds other values in their place, can miss the bound.
Values may be sent and summed in bfloat16 or wider, within the bound.
A program may use at most 128 MiB of HBM per device.

```python
import math
import jax
import jax.numpy as jnp
from jax import lax

D = 1024
H = 16
HD = 64
SEG = 128
QB = 128
OV = 8
QPD = 2
SPD = 8
NS = 32768
NG = 8192
NSEG = 256
NQB = 64
RL = 2048
N_REGION = 4
N_SEQ = 8


def layout_tables(key):
    seeded = jax.random.fold_in(key, 7101)
    key_perm, key_busy, key_popular, key_drawn, key_local, key_order = jax.random.split(seeded, 6)
    permuted = jax.random.permutation(key_perm, NSEG).astype(jnp.int32)
    inverse = jnp.argsort(permuted).astype(jnp.int32)
    heaviest_target = jax.random.randint(key_busy, (N_REGION, 1, 1, 1), 0, N_SEQ)
    frequent_targets = jax.random.randint(key_popular, (N_REGION, 1, 1, N_SEQ), 0, 1 << 20)
    sampled_picks = jax.random.randint(key_drawn, (N_REGION, N_SEQ, QPD, N_SEQ), 0, 1 << 20)
    destination_index = jnp.arange(N_SEQ, dtype=jnp.int32)
    extra_score_term = jnp.where(destination_index[None, None, None, :] == heaviest_target, 1 << 22, 0)
    logit_scores = (sampled_picks + frequent_targets + extra_score_term) * N_SEQ + destination_index[None, None, None, :]
    top_values, chosen = lax.top_k(logit_scores, OV)
    order_keys = jax.random.randint(key_order, (N_REGION, N_SEQ, QPD, OV), 0, 1 << 20) * OV + jnp.arange(OV, dtype=jnp.int32)
    shuffle = jnp.argsort(order_keys, axis=-1)
    chosen = jnp.take_along_axis(chosen, shuffle, axis=-1).astype(jnp.int32)
    local_slot = jax.random.randint(key_local, (N_REGION, N_SEQ, QPD, OV), 0, SPD)
    region_ids = jnp.arange(N_REGION, dtype=jnp.int32)[:, None, None, None]
    target = (region_ids * N_SEQ + chosen) * SPD + local_slot
    listed = jnp.take(inverse, target.reshape(NQB, OV), axis=0).astype(jnp.int32)
    return (permuted, listed)


def draw_seg_slot(key, part):
    return layout_tables(key)[0]


def draw_segment_lists(key, part):
    return layout_tables(key)[1]


def clipped_normal(key, dims):
    return jnp.clip(jax.random.normal(key, dims, dtype=jnp.float32), -6.0, 6.0) / math.sqrt(D)


def cross_pair(key):
    seeded = jax.random.fold_in(key, 7202)
    key_first, key_second = jax.random.split(seeded, 2)
    first = clipped_normal(key_first, (D, D))
    second = clipped_normal(key_second, (D, D))
    return (jnp.clip(first, -4.0, 4.0), jnp.clip(second, -4.0, 4.0))


def draw_query_weight(key, part):
    return cross_pair(key)[0].astype(jnp.bfloat16)


def draw_key_weight(key, part):
    return cross_pair(key)[1].astype(jnp.bfloat16)


def draw_packed_weight(key, part):
    seeded = jax.random.fold_in(key, 7303)
    key_query, key_keys, key_values = jax.random.split(seeded, 3)
    query_part = clipped_normal(key_query, (D, H, HD))
    value_part = clipped_normal(key_values, (D, H, HD))
    key_part = clipped_normal(key_keys, (D, H, HD))
    stacked = jnp.stack([query_part, key_part, value_part], axis=2).reshape(D, 3 * D)
    return jnp.clip(stacked, -4.0, 4.0).astype(jnp.bfloat16)


def shard_levels(rng, extent, cuts, low, high):
    loudness = 1.0
    for dim, shards_of in cuts:
        heights = jax.random.uniform(jax.random.fold_in(jax.random.fold_in(rng, 6), dim), (shards_of,), jnp.float32, low / len(cuts), high / len(cuts))
        loudness = loudness * jnp.repeat(jnp.exp(heights), extent[dim] // shards_of).reshape((-1,) + (1,) * (len(extent) - 1 - dim))
    return loudness


def normal_values(rng, shape, deviation, bound, shards=(), kind=jnp.bfloat16):
    drawn = jax.random.normal(rng, shape, jnp.float32) * deviation
    if len(shards) > 0:
        drawn = shard_levels(rng, shape, shards, -0.22, 0.18) * drawn
    return jnp.clip(drawn, min=-bound, max=bound).astype(kind)


def setup_inputs(seed: int = 0) -> dict:
    arg_keys = jax.random.split(jax.random.key(seed), 11)
    return {
        "scan_tokens": normal_values(arg_keys[0], (NS, D), 1.0, 6.0, ((0, 32),)),
        "grid_tokens": normal_values(arg_keys[1], (NG, D), 1.0, 6.0, ((0, 32),)),
        "seg_slot": draw_seg_slot(jax.random.fold_in(arg_keys[10], 71), 0),
        "segment_lists": draw_segment_lists(jax.random.fold_in(arg_keys[10], 71), 0),
        "query_weight": draw_query_weight(jax.random.fold_in(arg_keys[10], 71), 0),
        "key_weight": draw_key_weight(jax.random.fold_in(arg_keys[10], 71), 0),
        "value_weight": normal_values(arg_keys[6], (D, D), D ** -0.5, 0.1875),
        "mixer_weight": normal_values(arg_keys[7], (D, D), D ** -0.5, 0.1875),
        "packed_weight": draw_packed_weight(jax.random.fold_in(arg_keys[10], 71), 0),
        "merged_weight": normal_values(arg_keys[9], (D, D), D ** -0.5, 0.1875),
    }


norm_eps = 1e-06
masked_score = -1e+30

def rms_rows(values):
    widened = values.astype(jnp.float32)
    scaled = widened / jnp.sqrt(lax.optimization_barrier(jnp.mean(widened * widened, axis=-1, keepdims=True)) + norm_eps)
    return scaled.astype(jnp.bfloat16)

def pair_partials(queries, seg_keys, seg_values, head_count):
    pair_count, query_rows, model_width = queries.shape
    key_rows = seg_keys.shape[1]
    head_dim = model_width // head_count
    q_split = queries.reshape(pair_count, query_rows, head_count, head_dim).astype(jnp.float32)
    k_split = seg_keys.reshape(pair_count, key_rows, head_count, head_dim).astype(jnp.float32)
    v_split = seg_values.reshape(pair_count, key_rows, head_count, head_dim).astype(jnp.float32)
    logit_scores = jnp.einsum('bqhd,bkhd->bhqk', q_split, k_split) * (1.0 / math.sqrt(head_dim))
    maxima = lax.optimization_barrier(jnp.max(logit_scores, axis=-1))
    weights = jnp.exp(logit_scores - maxima[..., None])
    running_sums = lax.optimization_barrier(jnp.sum(weights, axis=-1))
    rounded = lax.optimization_barrier(weights.astype(jnp.bfloat16)).astype(jnp.float32)
    numerator = jnp.einsum('bhqk,bkhd->bqhd', rounded, v_split)
    return (numerator.reshape(pair_count, query_rows, model_width), maxima, running_sums)

def joined_pair_list(numerator, maxima, running_sums, live_pairs, head_count):
    live_mask = live_pairs[:, :, None, None]
    maxima = jnp.where(live_mask, maxima, masked_score)
    top_score = lax.optimization_barrier(jnp.max(maxima, axis=0))
    factors = jnp.where(live_mask, jnp.exp(maxima - top_score[None]), 0.0)
    denominator = lax.optimization_barrier(jnp.sum(factors * running_sums, axis=0))
    pair_count, block_count, query_rows, model_width = numerator.shape
    split_heads = numerator.reshape(pair_count, block_count, query_rows, head_count, model_width // head_count)
    summed = lax.optimization_barrier(jnp.sum(split_heads * jnp.swapaxes(factors, 2, 3)[..., None], axis=0))
    merged = summed / jnp.swapaxes(denominator, 1, 2)[..., None]
    return merged.reshape(block_count, query_rows, model_width).astype(jnp.bfloat16)

def region_attention(packed, heads_local, head_dim):
    row_count = packed.shape[0]
    queries = packed[:, :, 0].astype(jnp.float32)
    head_keys = packed[:, :, 1].astype(jnp.float32)
    head_values = packed[:, :, 2].astype(jnp.float32)
    step_rows = min(512, row_count)

    def one_block(query_part):
        logit_scores = jnp.einsum('qhd,khd->hqk', query_part, head_keys) * (1.0 / math.sqrt(head_dim))
        maxima = lax.optimization_barrier(jnp.max(logit_scores, axis=-1, keepdims=True))
        weights = jnp.exp(logit_scores - maxima)
        running_sums = lax.optimization_barrier(jnp.sum(weights, axis=-1))
        rounded = lax.optimization_barrier(weights.astype(jnp.bfloat16)).astype(jnp.float32)
        numerator = jnp.einsum('hqk,khd->qhd', rounded, head_values)
        return (numerator / jnp.transpose(running_sums)[..., None]).astype(jnp.bfloat16)
    blocks = lax.map(one_block, queries.reshape(row_count // step_rows, step_rows, heads_local, head_dim))
    return blocks.reshape(row_count, heads_local * head_dim)

def reference(scan_tokens, grid_tokens, seg_slot, segment_lists, query_weight, key_weight, value_weight, mixer_weight, packed_weight, merged_weight):
    scan_normed = rms_rows(scan_tokens)
    all_keys = jnp.dot(scan_normed, key_weight, preferred_element_type=jnp.float32).astype(jnp.bfloat16)
    all_values = jnp.dot(scan_normed, value_weight, preferred_element_type=jnp.float32).astype(jnp.bfloat16)
    queries = jnp.dot(rms_rows(grid_tokens), query_weight, preferred_element_type=jnp.float32).astype(jnp.bfloat16)
    queries = queries.reshape(NQB, QB, D)
    slots = jnp.take(seg_slot, segment_lists, axis=0).astype(jnp.int32)
    offsets = jnp.arange(SEG, dtype=jnp.int32)

    def one_block(element):
        block_queries, slot_row = element
        row_ids = (slot_row[:, None] * SEG + offsets[None, :]).astype(jnp.int32)
        seg_keys = jnp.take(all_keys, row_ids, axis=0)
        seg_values = jnp.take(all_values, row_ids, axis=0)
        spread = jnp.broadcast_to(block_queries[None], (OV, QB, D))
        numerator, maxima, running_sums = pair_partials(spread, seg_keys, seg_values, H)
        live_pairs = jnp.ones((OV, 1), dtype=bool)
        return joined_pair_list(numerator[:, None], maxima[:, None], running_sums[:, None], live_pairs, H)[0]
    cross = lax.map(one_block, (queries, slots)).reshape(NG, D)
    mixed = (grid_tokens.astype(jnp.float32) + jnp.dot(cross, mixer_weight, preferred_element_type=jnp.float32)).astype(jnp.bfloat16)
    packed = jnp.dot(rms_rows(mixed), packed_weight, preferred_element_type=jnp.float32).astype(jnp.bfloat16)
    packed = packed.reshape(N_REGION, RL, H, 3, HD)

    def one_region(region_packed):
        per_head = jnp.transpose(region_packed, (1, 0, 2, 3))[:, :, None]
        outputs = lax.map(lambda head_packed: region_attention(head_packed, 1, HD), per_head)
        return jnp.transpose(outputs, (1, 0, 2)).reshape(RL, H * HD)
    attended = lax.map(one_region, packed).reshape(NG, D)
    return (mixed.astype(jnp.float32) + jnp.dot(attended, merged_weight, preferred_element_type=jnp.float32)).astype(jnp.bfloat16)
```

```python
import functools
import math

import jax
import jax.numpy as jnp
from jax import lax
from jax.experimental import pallas as pl
from jax.experimental.pallas import tpu as pltpu
from jax.sharding import PartitionSpec as P

H = 16
SEG = 128

norm_eps = 1e-06
masked_score = -1e30
MESH = pl.DeviceIdType.MESH
VMEM_BYTES = 56 * 1024 * 1024


def rms_f32(widened):
    return widened / jnp.sqrt(jnp.mean(widened * widened, axis=-1, keepdims=True) + norm_eps)


def rms_rows(values):
    return rms_f32(values.astype(jnp.float32)).astype(jnp.bfloat16)


def stride_for(count):
    return 3 if math.gcd(3, count) == 1 else 1


def index_kernel(n_reg, n_seq, in_ref, out_ref, send_sem, recv_sem, send_sem2, recv_sem2):
    reg, seq = lax.axis_index("region"), lax.axis_index("seq")
    barrier = pltpu.get_barrier_semaphore()
    for k in range(1, n_reg):
        pl.semaphore_signal(
            barrier, inc=1, device_id=(lax.rem(reg + k, n_reg), seq), device_id_type=MESH
        )
    for k in range(1, n_seq):
        pl.semaphore_signal(
            barrier, inc=1, device_id=(reg, lax.rem(seq + k, n_seq)), device_id_type=MESH
        )
    out_ref[seq, reg] = in_ref[...]
    pl.semaphore_wait(barrier, n_reg + n_seq - 2)

    def over_region(k):
        return pltpu.make_async_remote_copy(
            src_ref=in_ref,
            dst_ref=out_ref.at[seq, reg],
            send_sem=send_sem.at[k],
            recv_sem=recv_sem.at[k],
            device_id=(lax.rem(reg + k, n_reg), seq),
            device_id_type=MESH,
        )

    for k in range(1, n_reg):
        over_region(k).start()
    for k in range(1, n_reg):
        over_region(k).wait()

    def over_seq(k):
        return pltpu.make_async_remote_copy(
            src_ref=out_ref.at[seq],
            dst_ref=out_ref.at[seq],
            send_sem=send_sem2.at[k],
            recv_sem=recv_sem2.at[k],
            device_id=(reg, lax.rem(seq + k, n_seq)),
            device_id_type=MESH,
        )

    for k in range(1, n_seq):
        over_seq(k).start()
    for k in range(1, n_seq):
        over_seq(k).wait()


def gather_indices(packed, n_reg, n_seq):
    return pl.pallas_call(
        functools.partial(index_kernel, n_reg, n_seq),
        out_shape=jax.ShapeDtypeStruct((n_seq, n_reg) + packed.shape, jnp.int32),
        in_specs=[pl.BlockSpec(memory_space=pltpu.VMEM)],
        out_specs=pl.BlockSpec(memory_space=pltpu.VMEM),
        scratch_shapes=[
            pltpu.SemaphoreType.DMA((n_reg,)),
            pltpu.SemaphoreType.DMA((n_reg,)),
            pltpu.SemaphoreType.DMA((n_seq,)),
            pltpu.SemaphoreType.DMA((n_seq,)),
        ],
        compiler_params=pltpu.CompilerParams(collective_id=0, has_side_effects=True),
    )(packed)


def cross_kernel(
    n, blocks, pairs, head_dim, all_live,
    pick_ref, live_ref, scan_ref, grid_ref, wq_hbm, wk_hbm, wv_hbm,
    out_ref,
    wq, wk, wv, send, recv, qm, ks, vs, top, total, acc,
    w_sem, send_sem, recv_sem,
):
    reg, me = lax.axis_index("region"), lax.axis_index("seq")
    stride = stride_for(n)
    loads = [
        pltpu.make_async_copy(src, dst, w_sem.at[i])
        for i, (src, dst) in enumerate(((wq_hbm, wq), (wk_hbm, wk), (wv_hbm, wv)))
    ]
    for load in loads:
        load.start()
    barrier = pltpu.get_barrier_semaphore()
    for k in range(1, n):
        pl.semaphore_signal(
            barrier, inc=1, device_id=(reg, lax.rem(me + k, n)), device_id_type=MESH
        )
    pl.semaphore_wait(barrier, n - 1)

    def copy(i):
        return pltpu.make_async_remote_copy(
            src_ref=send.at[i],
            dst_ref=recv.at[i],
            send_sem=send_sem.at[i],
            recv_sem=recv_sem.at[i],
            device_id=(reg, lax.rem(me + stride * i, n)),
            device_id_type=MESH,
        )

    def stage(i, carry):
        for b in range(blocks):
            send[i, b * SEG : (b + 1) * SEG] = rms_rows(scan_ref[pick_ref[i, b]])
        copy(i).start()
        return carry

    lax.fori_loop(1, n, stage, 0)
    for b in range(blocks):
        recv[0, b * SEG : (b + 1) * SEG] = rms_rows(scan_ref[pick_ref[0, b]])

    rows = grid_ref.shape[0] // blocks
    width = 2 * head_dim
    low = lax.broadcasted_iota(jnp.int32, (rows, width), 1) < head_dim
    loads[0].wait()
    scale = 1.0 / math.sqrt(head_dim)
    queries = jnp.dot(rms_rows(grid_ref[...]), wq[...], preferred_element_type=jnp.float32)
    queries = queries.astype(jnp.bfloat16).astype(jnp.float32) * scale
    for b in range(blocks):
        for p in range(pairs):
            part = queries[b * rows : (b + 1) * rows, p * width : (p + 1) * width]
            j = b * pairs + p
            qm[j, :rows] = jnp.where(low, part, 0.0).astype(jnp.bfloat16)
            qm[j, rows:] = jnp.where(low, 0.0, part).astype(jnp.bfloat16)
    top[...] = jnp.full(top.shape, masked_score, jnp.float32)
    total[...] = jnp.zeros(total.shape, jnp.float32)
    acc[...] = jnp.zeros(acc.shape, jnp.float32)
    for p in range(pairs):
        vs[p, :, width:] = jnp.ones((blocks * SEG, width), jnp.bfloat16)
    loads[1].wait()
    loads[2].wait()

    def process(i, carry):
        @pl.when(i > 0)
        def _():
            copy(i).wait_recv()

        arrived = recv[i]
        keys = jnp.dot(arrived, wk[...], preferred_element_type=jnp.float32).astype(jnp.bfloat16)
        for p in range(pairs):
            ks[p] = keys[:, p * width : (p + 1) * width]
        vals = jnp.dot(arrived, wv[...], preferred_element_type=jnp.float32).astype(jnp.bfloat16)
        for p in range(pairs):
            vs[p, :, :width] = vals[:, p * width : (p + 1) * width]

        for b in range(blocks):
            at = slice(b * SEG, (b + 1) * SEG)

            def attend(p, b, at):
                j = b * pairs + p
                scores = lax.dot_general(
                    qm[j], ks[p, at], (((1,), (1,)), ((), ())), preferred_element_type=jnp.float32
                )
                if not all_live:
                    scores = jnp.where(live_ref[i, b] > 0, scores, masked_score)
                old = top[j]
                new = jnp.maximum(old, jnp.max(scores, axis=-1, keepdims=True))
                weights = jnp.exp(scores - new).astype(jnp.bfloat16)
                factor = jnp.exp(old - new)
                factor = jnp.where(low, factor[:rows], factor[rows:])
                summed = jnp.dot(weights, vs[p, at], preferred_element_type=jnp.float32)
                acc[j] = acc[j] * factor + jnp.where(low, summed[:rows, :width], summed[rows:, :width])
                total[j] = total[j] * factor + jnp.where(
                    low, summed[:rows, width:], summed[rows:, width:]
                )
                top[j] = new

            def four(g, inner, b=b, at=at):
                for u in range(4):
                    attend(g * 4 + u, b, at)
                return inner

            lax.fori_loop(0, pairs // 4, four, 0)
        return carry

    lax.fori_loop(0, n, process, 0)
    for b in range(blocks):
        for p in range(pairs):
            j = b * pairs + p
            out_ref[b * rows : (b + 1) * rows, p * width : (p + 1) * width] = (
                acc[j] / total[j]
            ).astype(jnp.bfloat16)

    def finish(i, carry):
        copy(i).wait_send()
        return carry

    lax.fori_loop(1, n, finish, 0)


def cross_attention(pick, live, scan, grid_tokens, wq, wk, wv, n, blocks, all_live):
    rows, model = grid_tokens.shape
    head_dim = model // H
    pairs = H // 2
    width = 2 * head_dim
    block_rows = rows // blocks
    vmem = pl.BlockSpec(memory_space=pltpu.VMEM)
    smem = pl.BlockSpec(memory_space=pltpu.SMEM)
    hbm = pl.BlockSpec(memory_space=pl.ANY)
    weight = pltpu.VMEM((model, model), jnp.bfloat16)
    return pl.pallas_call(
        functools.partial(cross_kernel, n, blocks, pairs, head_dim, all_live),
        out_shape=jax.ShapeDtypeStruct((rows, model), jnp.bfloat16),
        in_specs=[smem, smem, vmem, vmem, hbm, hbm, hbm],
        out_specs=vmem,
        scratch_shapes=[
            weight,
            weight,
            weight,
            pltpu.VMEM((n, blocks * SEG, model), jnp.bfloat16),
            pltpu.VMEM((n, blocks * SEG, model), jnp.bfloat16),
            pltpu.VMEM((blocks * pairs, 2 * block_rows, width), jnp.bfloat16),
            pltpu.VMEM((pairs, blocks * SEG, width), jnp.bfloat16),
            pltpu.VMEM((pairs, blocks * SEG, 2 * width), jnp.bfloat16),
            pltpu.VMEM((blocks * pairs, 2 * block_rows, SEG), jnp.float32),
            pltpu.VMEM((blocks * pairs, block_rows, width), jnp.float32),
            pltpu.VMEM((blocks * pairs, block_rows, width), jnp.float32),
            pltpu.SemaphoreType.DMA((3,)),
            pltpu.SemaphoreType.DMA((n,)),
            pltpu.SemaphoreType.DMA((n,)),
        ],
        compiler_params=pltpu.CompilerParams(
            collective_id=1, has_side_effects=True, vmem_limit_bytes=VMEM_BYTES
        ),
    )(pick, live, scan, grid_tokens, wq, wk, wv)


def region_kernel(
    n, heads, head_dim, packed_ref, out_ref,
    took, ks, vs, made, got, send_sem, recv_sem, send_sem2, recv_sem2,
):
    reg, me = lax.axis_index("region"), lax.axis_index("seq")
    stride = stride_for(n)
    rows = packed_ref.shape[1]
    barrier = pltpu.get_barrier_semaphore()
    for k in range(1, n):
        pl.semaphore_signal(
            barrier, inc=1, device_id=(reg, lax.rem(me + k, n)), device_id_type=MESH
        )
    pl.semaphore_wait(barrier, n - 1)

    def outward(i):
        to = lax.rem(me + stride * i, n)
        return pltpu.make_async_remote_copy(
            src_ref=packed_ref.at[to],
            dst_ref=took.at[me],
            send_sem=send_sem.at[i],
            recv_sem=recv_sem.at[i],
            device_id=(reg, to),
            device_id_type=MESH,
        )

    def inward(i):
        source = lax.rem(me + (n * stride - stride * i), n)
        return pltpu.make_async_remote_copy(
            src_ref=packed_ref.at[source],
            dst_ref=took.at[source],
            send_sem=send_sem.at[i],
            recv_sem=recv_sem.at[i],
            device_id=(reg, source),
            device_id_type=MESH,
        )

    def back(i):
        to = lax.rem(me + stride * i, n)
        return pltpu.make_async_remote_copy(
            src_ref=made.at[i],
            dst_ref=got.at[me],
            send_sem=send_sem2.at[i],
            recv_sem=recv_sem2.at[i],
            device_id=(reg, to),
            device_id_type=MESH,
        )

    def back_in(i):
        source = lax.rem(me + (n * stride - stride * i), n)
        return pltpu.make_async_remote_copy(
            src_ref=made.at[i],
            dst_ref=got.at[source],
            send_sem=send_sem2.at[i],
            recv_sem=recv_sem2.at[i],
            device_id=(reg, source),
            device_id_type=MESH,
        )

    def each(first, last, body):
        def step(i, carry):
            body(i)
            return carry

        lax.fori_loop(first, last, step, 0)

    each(1, n, lambda i: outward(i).start())

    def place(source):
        part = took[source]
        at = pl.ds(pl.multiple_of(source * rows, rows), rows)
        for h in range(heads):
            base = 3 * h * head_dim
            ks[h, at, :] = part[:, base + head_dim : base + 2 * head_dim]
            vs[h, at, :head_dim] = part[:, base + 2 * head_dim : base + 3 * head_dim]

    for h in range(heads):
        vs[h, :, head_dim:] = jnp.ones((n * rows, head_dim), jnp.bfloat16)
    took[me] = packed_ref[me]
    place(me)

    def arrive(i):
        inward(i).wait_recv()
        place(lax.rem(me + (n * stride - stride * i), n))

    each(1, n, arrive)
    scale = 1.0 / math.sqrt(head_dim)

    def attend(i):
        to = lax.rem(me + stride * i, n)
        part = took[to]
        for h in range(heads):
            base = 3 * h * head_dim
            q = part[:, base : base + head_dim] * jnp.bfloat16(scale)
            scores = lax.dot_general(
                q, ks[h], (((1,), (1,)), ((), ())), preferred_element_type=jnp.float32
            )
            peak = jnp.max(scores, axis=-1, keepdims=True)
            weights = jnp.exp(scores - peak).astype(jnp.bfloat16)
            summed = jnp.dot(weights, vs[h], preferred_element_type=jnp.float32)
            made[i, :, h * head_dim : (h + 1) * head_dim] = (
                summed[:, :head_dim] / summed[:, head_dim:]
            ).astype(jnp.bfloat16)

    def attend_send(i):
        attend(i)
        back(i).start()

    each(1, n, attend_send)
    attend(0)
    got[me] = made[0]
    each(1, n, lambda i: back_in(i).wait_recv())
    span = heads * head_dim
    for s in range(n):
        out_ref[:, s * span : (s + 1) * span] = got[s]
    each(1, n, lambda i: outward(i).wait_send())
    each(1, n, lambda i: back(i).wait_send())


def region_attention(packed, n):
    _, rows, columns = packed.shape
    heads = H // n
    head_dim = columns // (3 * heads)
    span = heads * head_dim
    vmem = pl.BlockSpec(memory_space=pltpu.VMEM)
    return pl.pallas_call(
        functools.partial(region_kernel, n, heads, head_dim),
        out_shape=jax.ShapeDtypeStruct((rows, n * span), jnp.bfloat16),
        in_specs=[vmem],
        out_specs=vmem,
        scratch_shapes=[
            pltpu.VMEM((n, rows, columns), jnp.bfloat16),
            pltpu.VMEM((heads, n * rows, head_dim), jnp.bfloat16),
            pltpu.VMEM((heads, n * rows, 2 * head_dim), jnp.bfloat16),
            pltpu.VMEM((n, rows, span), jnp.bfloat16),
            pltpu.VMEM((n, rows, span), jnp.bfloat16),
            pltpu.SemaphoreType.DMA((n,)),
            pltpu.SemaphoreType.DMA((n,)),
            pltpu.SemaphoreType.DMA((n,)),
            pltpu.SemaphoreType.DMA((n,)),
        ],
        compiler_params=pltpu.CompilerParams(
            collective_id=2, has_side_effects=True, vmem_limit_bytes=VMEM_BYTES
        ),
    )(packed)


def on_device(
    scan_tokens,
    grid_tokens,
    seg_slot,
    segment_lists,
    query_weight,
    key_weight,
    value_weight,
    mixer_weight,
    packed_weight,
    merged_weight,
):
    n_reg, n = lax.axis_size("region"), lax.axis_size("seq")
    reg, me = lax.axis_index("region"), lax.axis_index("seq")
    model_width = scan_tokens.shape[1]
    seg_local = scan_tokens.shape[0] // SEG
    blocks, overlap = segment_lists.shape
    rows = grid_tokens.shape[0]

    flat = jnp.concatenate([seg_slot, segment_lists.reshape(-1)])
    used = flat.shape[0]
    tiles = -(-used // 1024)
    flat = jnp.pad(flat, (0, tiles * 1024 - used)).reshape(tiles * 8, 128)
    tables = gather_indices(flat, n_reg, n).reshape(n, n_reg, tiles * 1024)
    all_slots = jnp.swapaxes(tables[:, :, :seg_local], 0, 1).reshape(-1)
    lists = lax.dynamic_index_in_dim(tables, reg, axis=1, keepdims=False)
    lists = lists[:, seg_local:used].reshape(n, blocks, overlap)
    numbers = jnp.arange(all_slots.shape[0], dtype=jnp.int32)
    wanted = jnp.sum(jnp.where(lists[..., None] == numbers, all_slots, 0), axis=-1)
    wanted = wanted - reg * (n * seg_local)
    mine = wanted // seg_local == me
    pick = jnp.sum(jnp.where(mine, wanted % seg_local, 0), axis=-1)
    steps = stride_for(n) * jnp.arange(n, dtype=jnp.int32)
    pick = jnp.take(pick, (me + steps) % n, axis=0, mode="clip")
    all_live = overlap == n
    if all_live:
        live = jnp.ones((n, blocks), jnp.int32)
    else:
        own = lax.dynamic_index_in_dim(wanted, me, axis=0, keepdims=False) // seg_local
        sources = (me - steps) % n
        live = jnp.any(own[None] == sources[:, None, None], axis=-1).astype(jnp.int32)

    cross = cross_attention(
        pick, live, scan_tokens.reshape(seg_local, SEG, model_width), grid_tokens,
        query_weight, key_weight, value_weight, n, blocks, all_live,
    )
    mixed = (
        grid_tokens.astype(jnp.float32)
        + jnp.dot(cross, mixer_weight, preferred_element_type=jnp.float32)
    ).astype(jnp.bfloat16)
    packed = jnp.dot(rms_rows(mixed), packed_weight, preferred_element_type=jnp.float32).astype(
        jnp.bfloat16
    )
    returned = region_attention(jnp.swapaxes(packed.reshape(rows, n, -1), 0, 1), n)
    return (
        mixed.astype(jnp.float32)
        + jnp.dot(returned, merged_weight, preferred_element_type=jnp.float32)
    ).astype(jnp.bfloat16)


def solution(mesh):
    in_specs = (
        P(("region", "seq"), None),
        P(("region", "seq"), None),
        P(("region", "seq")),
        P(("region", "seq"), None),
        P(),
        P(),
        P(),
        P(),
        P(),
        P(),
    )
    out_specs = P(("region", "seq"), None)
    return jax.shard_map(
        on_device, mesh=mesh, in_specs=in_specs, out_specs=out_specs, check_vma=False
    )
```

```python
import functools
import math

import jax
import jax.numpy as jnp
from jax import lax
from jax.experimental import pallas as pl
from jax.experimental.pallas import tpu as pltpu
from jax.sharding import PartitionSpec as P

H = 16
SEG = 128

norm_eps = 1e-06
masked_score = -1e30
MESH = pl.DeviceIdType.MESH
VMEM_BYTES = 56 * 1024 * 1024


def rms_f32(widened):
    return widened / jnp.sqrt(jnp.mean(widened * widened, axis=-1, keepdims=True) + norm_eps)


def rms_rows(values):
    return rms_f32(values.astype(jnp.float32)).astype(jnp.bfloat16)


def stride_for(count):
    return 3 if math.gcd(3, count) == 1 else 1


def index_kernel(n_reg, n_seq, in_ref, out_ref, send_sem, recv_sem, send_sem2, recv_sem2):
    reg, seq = lax.axis_index("region"), lax.axis_index("seq")
    barrier = pltpu.get_barrier_semaphore()
    for k in range(1, n_reg):
        pl.semaphore_signal(
            barrier, inc=1, device_id=(lax.rem(reg + k, n_reg), seq), device_id_type=MESH
        )
    for k in range(1, n_seq):
        pl.semaphore_signal(
            barrier, inc=1, device_id=(reg, lax.rem(seq + k, n_seq)), device_id_type=MESH
        )
    out_ref[seq, reg] = in_ref[...]
    pl.semaphore_wait(barrier, n_reg + n_seq - 2)

    def over_region(k):
        return pltpu.make_async_remote_copy(
            src_ref=in_ref,
            dst_ref=out_ref.at[seq, reg],
            send_sem=send_sem.at[k],
            recv_sem=recv_sem.at[k],
            device_id=(lax.rem(reg + k, n_reg), seq),
            device_id_type=MESH,
        )

    for k in range(1, n_reg):
        over_region(k).start()
    for k in range(1, n_reg):
        over_region(k).wait()

    def over_seq(k):
        return pltpu.make_async_remote_copy(
            src_ref=out_ref.at[seq],
            dst_ref=out_ref.at[seq],
            send_sem=send_sem2.at[k],
            recv_sem=recv_sem2.at[k],
            device_id=(reg, lax.rem(seq + k, n_seq)),
            device_id_type=MESH,
        )

    for k in range(1, n_seq):
        over_seq(k).start()
    for k in range(1, n_seq):
        over_seq(k).wait()


def gather_indices(packed, n_reg, n_seq):
    return pl.pallas_call(
        functools.partial(index_kernel, n_reg, n_seq),
        out_shape=jax.ShapeDtypeStruct((n_seq, n_reg) + packed.shape, jnp.int32),
        in_specs=[pl.BlockSpec(memory_space=pltpu.VMEM)],
        out_specs=pl.BlockSpec(memory_space=pltpu.VMEM),
        scratch_shapes=[
            pltpu.SemaphoreType.DMA((n_reg,)),
            pltpu.SemaphoreType.DMA((n_reg,)),
            pltpu.SemaphoreType.DMA((n_seq,)),
            pltpu.SemaphoreType.DMA((n_seq,)),
        ],
        compiler_params=pltpu.CompilerParams(collective_id=0, has_side_effects=True),
    )(packed)


def group_bounds(n):
    return [(0, n)]


def region_phase(
    n, reg, me, heads, head_dim, rows, snd, out_ref,
    took, ks, vs, top, acc, made, got, send_sem, recv_sem, send_sem2, recv_sem2,
):
    stride = stride_for(n)

    def ahead(i):
        return lax.rem(me + stride * i, n)

    def behind(i):
        return lax.rem(me + (n * stride - stride * i), n)

    def outward(i):
        return pltpu.make_async_remote_copy(
            src_ref=snd.at[ahead(i)],
            dst_ref=took.at[i],
            send_sem=send_sem.at[i],
            recv_sem=recv_sem.at[i],
            device_id=(reg, ahead(i)),
            device_id_type=MESH,
        )

    def back(i):
        return pltpu.make_async_remote_copy(
            src_ref=made.at[i],
            dst_ref=got.at[me],
            send_sem=send_sem2.at[i],
            recv_sem=recv_sem2.at[i],
            device_id=(reg, behind(i)),
            device_id_type=MESH,
        )

    def back_in(i):
        return pltpu.make_async_remote_copy(
            src_ref=made.at[i],
            dst_ref=got.at[ahead(i)],
            send_sem=send_sem2.at[i],
            recv_sem=recv_sem2.at[i],
            device_id=(reg, ahead(i)),
            device_id_type=MESH,
        )

    def each(first, last, body):
        def step(i, carry):
            body(i)
            return carry

        lax.fori_loop(first, last, step, 0)

    each(1, n, lambda i: outward(i).start())
    for h in range(heads):
        vs[h, :, head_dim:] = jnp.ones((n * rows, head_dim), jnp.bfloat16)
    took[0] = snd[me]
    scale = 1.0 / math.sqrt(head_dim)

    def place(i):
        at = slice(i * rows, (i + 1) * rows)
        for h in range(heads):
            base = 3 * h * head_dim
            ks[h, at, :] = took[i, :, base + head_dim : base + 2 * head_dim]
            vs[h, at, :head_dim] = took[i, :, base + 2 * head_dim : base + 3 * head_dim]

    def scores_of(i, h, at, own=slice(None)):
        base = 3 * h * head_dim
        q = took[i, own, base : base + head_dim] * jnp.bfloat16(scale)
        return lax.dot_general(
            q, ks[h, at], (((1,), (1,)), ((), ())), preferred_element_type=jnp.float32
        )

    def finish(i, h, summed, own=slice(None)):
        made[i, own, h * head_dim : (h + 1) * head_dim] = (
            summed[:, :head_dim] / summed[:, head_dim:]
        ).astype(jnp.bfloat16)

    for low, high in group_bounds(n):
        for i in range(low, high):
            if i > 0:
                outward(i).wait_recv()
            place(i)
        last = high == n

        def older(i, low=low, high=high, last=last):
            at = slice(low * rows, high * rows)
            for h in range(heads):
                scores = scores_of(i, h, at)
                old = top[h * n + i]
                new = jnp.maximum(old, jnp.max(scores, axis=-1, keepdims=True))
                weights = jnp.exp((scores - new[:, :1]).astype(jnp.bfloat16))
                summed = jnp.dot(weights, vs[h, at], preferred_element_type=jnp.float32)
                summed = acc[h * n + i] * jnp.exp(old - new) + summed
                if last:
                    finish(i, h, summed)
                else:
                    acc[h * n + i] = summed
                    top[h * n + i] = new

        def fresh(i, low=low, high=high, last=last):
            at = slice(0, high * rows)
            parts = max(1, high * rows // 2048)
            for h in range(heads):
                for part in range(parts):
                    own = slice(part * rows // parts, (part + 1) * rows // parts)
                    scores = scores_of(i, h, at, own)
                    peak = jnp.max(scores, axis=-1, keepdims=True)
                    weights = jnp.exp((scores - peak).astype(jnp.bfloat16))
                    summed = jnp.dot(weights, vs[h, at], preferred_element_type=jnp.float32)
                    if last:
                        finish(i, h, summed, own)
                    else:
                        acc[h * n + i, own] = summed
                        top[h * n + i, own] = jnp.broadcast_to(peak, summed.shape)

        if last:
            def fresh_send(i, fresh=fresh):
                fresh(i)
                back(i).start()

            def older_send(i, older=older):
                older(i)
                back(i).start()

            each(max(low, 1), high, fresh_send)
            each(1, low, older_send)
            if low > 0:
                each(0, 1, older)
            else:
                each(0, 1, fresh)
        else:
            each(0, low, older)
            each(low, high, fresh)

    got[me] = made[0]
    each(1, n, lambda i: back_in(i).wait_recv())
    span = heads * head_dim
    for s in range(n):
        out_ref[:, s * span : (s + 1) * span] = got[s]
    each(1, n, lambda i: outward(i).wait_send())
    each(1, n, lambda i: back(i).wait_send())


def cross_kernel(
    n, blocks, pairs, head_dim, all_live,
    pick_ref, live_ref, scan_ref, grid_ref, wq_hbm, wk_hbm, wv_hbm, wm_hbm, wp_hbm,
    mixed_ref, out_ref,
    wq, wk, wv, wm, wp, send, recv, qm, ks, vs, top, sums, cross,
    snd, took, region_ks, region_vs, made, got,
    w_sem, send_sem, recv_sem, out_send, out_recv, back_send, back_recv,
):
    reg, me = lax.axis_index("region"), lax.axis_index("seq")
    stride = stride_for(n)
    weight_pairs = (
        (wq_hbm, wq), (wk_hbm, wk), (wv_hbm, wv), (wm_hbm, wm), (wp_hbm, wp)
    )
    loads = [
        pltpu.make_async_copy(src, dst, w_sem.at[i])
        for i, (src, dst) in enumerate(weight_pairs)
    ]
    for load in loads:
        load.start()
    barrier = pltpu.get_barrier_semaphore()
    for k in range(1, n):
        pl.semaphore_signal(
            barrier, inc=1, device_id=(reg, lax.rem(me + k, n)), device_id_type=MESH
        )
    pl.semaphore_wait(barrier, n - 1)

    def copy(i):
        return pltpu.make_async_remote_copy(
            src_ref=send.at[i],
            dst_ref=recv.at[i],
            send_sem=send_sem.at[i],
            recv_sem=recv_sem.at[i],
            device_id=(reg, lax.rem(me + stride * i, n)),
            device_id_type=MESH,
        )

    def stage(i, carry):
        for b in range(blocks):
            send[i, b * SEG : (b + 1) * SEG] = rms_rows(scan_ref[pick_ref[i, b]])
        copy(i).start()
        return carry

    lax.fori_loop(1, n, stage, 0)
    for b in range(blocks):
        recv[0, b * SEG : (b + 1) * SEG] = rms_rows(scan_ref[pick_ref[0, b]])

    rows = grid_ref.shape[0] // blocks
    width = 2 * head_dim
    low = lax.broadcasted_iota(jnp.int32, (rows, width), 1) < head_dim
    loads[0].wait()
    scale = 1.0 / math.sqrt(head_dim)
    queries = jnp.dot(rms_rows(grid_ref[...]), wq[...], preferred_element_type=jnp.float32)
    queries = queries.astype(jnp.bfloat16).astype(jnp.float32) * scale
    for b in range(blocks):
        for p in range(pairs):
            part = queries[b * rows : (b + 1) * rows, p * width : (p + 1) * width]
            j = b * pairs + p
            qm[j, :rows] = jnp.where(low, part, 0.0).astype(jnp.bfloat16)
            qm[j, rows:] = jnp.where(low, 0.0, part).astype(jnp.bfloat16)
    top[...] = jnp.full(top.shape, masked_score, jnp.float32)
    sums[...] = jnp.zeros(sums.shape, jnp.float32)
    for p in range(pairs):
        vs[p, :, width:] = jnp.ones((blocks * SEG, width), jnp.bfloat16)
    loads[1].wait()
    loads[2].wait()

    def process(i, carry):
        @pl.when(i > 0)
        def _():
            copy(i).wait_recv()

        arrived = recv[i]
        keys = jnp.dot(arrived, wk[...], preferred_element_type=jnp.float32).astype(jnp.bfloat16)
        for p in range(pairs):
            ks[p] = keys[:, p * width : (p + 1) * width]
        vals = jnp.dot(arrived, wv[...], preferred_element_type=jnp.float32).astype(jnp.bfloat16)
        for p in range(pairs):
            vs[p, :, :width] = vals[:, p * width : (p + 1) * width]

        for b in range(blocks):
            at = slice(b * SEG, (b + 1) * SEG)

            def attend(p, b, at):
                j = b * pairs + p
                scores = lax.dot_general(
                    qm[j], ks[p, at], (((1,), (1,)), ((), ())), preferred_element_type=jnp.float32
                )
                if not all_live:
                    scores = jnp.where(live_ref[i, b] > 0, scores, masked_score)
                old = top[j]
                new = jnp.maximum(old, jnp.max(scores, axis=-1, keepdims=True))
                weights = jnp.exp(scores - new).astype(jnp.bfloat16)
                factor = jnp.exp(old - new)
                factor = jnp.where(low, factor[:rows], factor[rows:])
                summed = jnp.dot(weights, vs[p, at], preferred_element_type=jnp.float32)
                sums[j, :rows] = sums[j, :rows] * factor + jnp.where(low, summed[:rows, :width], summed[rows:, :width])
                sums[j, rows:] = sums[j, rows:] * factor + jnp.where(
                    low, summed[:rows, width:], summed[rows:, width:]
                )
                top[j] = new

            def four(g, inner, b=b, at=at):
                for u in range(4):
                    attend(g * 4 + u, b, at)
                return inner

            lax.fori_loop(0, pairs // 4, four, 0)
        return carry

    lax.fori_loop(0, n, process, 0)
    for b in range(blocks):
        for p in range(pairs):
            j = b * pairs + p
            cross[b * rows : (b + 1) * rows, p * width : (p + 1) * width] = (
                sums[j, :rows] / sums[j, rows:]
            ).astype(jnp.bfloat16)

    loads[3].wait()
    loads[4].wait()
    mixed = (
        grid_ref[...].astype(jnp.float32)
        + jnp.dot(cross[...], wm[...], preferred_element_type=jnp.float32)
    ).astype(jnp.bfloat16)
    mixed_ref[...] = mixed
    normed = rms_rows(mixed)
    share = snd.shape[2]
    for d in range(n):
        snd[d] = jnp.dot(
            normed, wp[:, d * share : (d + 1) * share], preferred_element_type=jnp.float32
        ).astype(jnp.bfloat16)
    region_phase(
        n, reg, me, 2 * pairs // n, head_dim, grid_ref.shape[0], snd, out_ref, took, region_ks,
        region_vs, top, sums, made, got, out_send, out_recv, back_send, back_recv,
    )

    def finish(i, carry):
        copy(i).wait_send()
        return carry

    lax.fori_loop(1, n, finish, 0)


def both_attentions(pick, live, scan, grid_tokens, weights, n, blocks, all_live):
    rows, model = grid_tokens.shape
    head_dim = model // H
    pairs = H // 2
    width = 2 * head_dim
    block_rows = rows // blocks
    heads = H // n
    span = heads * head_dim
    vmem = pl.BlockSpec(memory_space=pltpu.VMEM)
    smem = pl.BlockSpec(memory_space=pltpu.SMEM)
    hbm = pl.BlockSpec(memory_space=pl.ANY)
    weight = pltpu.VMEM((model, model), jnp.bfloat16)
    return pl.pallas_call(
        functools.partial(cross_kernel, n, blocks, pairs, head_dim, all_live),
        out_shape=(jax.ShapeDtypeStruct((rows, model), jnp.bfloat16),) * 2,
        in_specs=[smem, smem, vmem, vmem] + [hbm] * 5,
        out_specs=(vmem, vmem),
        scratch_shapes=[
            weight,
            weight,
            weight,
            weight,
            pltpu.VMEM((model, 3 * model), jnp.bfloat16),
            pltpu.VMEM((n, blocks * SEG, model), jnp.bfloat16),
            pltpu.VMEM((n, blocks * SEG, model), jnp.bfloat16),
            pltpu.VMEM((blocks * pairs, 2 * block_rows, width), jnp.bfloat16),
            pltpu.VMEM((pairs, blocks * SEG, width), jnp.bfloat16),
            pltpu.VMEM((pairs, blocks * SEG, 2 * width), jnp.bfloat16),
            pltpu.VMEM((blocks * pairs, 2 * block_rows, SEG), jnp.float32),
            pltpu.VMEM((blocks * pairs, 2 * block_rows, width), jnp.float32),
            pltpu.VMEM((rows, model), jnp.bfloat16),
            pltpu.VMEM((n, rows, 3 * span), jnp.bfloat16),
            pltpu.VMEM((n, rows, 3 * span), jnp.bfloat16),
            pltpu.VMEM((heads, n * rows, head_dim), jnp.bfloat16),
            pltpu.VMEM((heads, n * rows, 2 * head_dim), jnp.bfloat16),
            pltpu.VMEM((n, rows, span), jnp.bfloat16),
            pltpu.VMEM((n, rows, span), jnp.bfloat16),
            pltpu.SemaphoreType.DMA((5,)),
        ] + [pltpu.SemaphoreType.DMA((n,))] * 6,
        compiler_params=pltpu.CompilerParams(
            collective_id=1, has_side_effects=True, vmem_limit_bytes=VMEM_BYTES
        ),
    )(pick, live, scan, grid_tokens, *weights)


def on_device(
    scan_tokens,
    grid_tokens,
    seg_slot,
    segment_lists,
    query_weight,
    key_weight,
    value_weight,
    mixer_weight,
    packed_weight,
    merged_weight,
):
    n_reg, n = lax.axis_size("region"), lax.axis_size("seq")
    reg, me = lax.axis_index("region"), lax.axis_index("seq")
    model_width = scan_tokens.shape[1]
    seg_local = scan_tokens.shape[0] // SEG
    blocks, overlap = segment_lists.shape

    flat = jnp.concatenate([seg_slot, segment_lists.reshape(-1)])
    used = flat.shape[0]
    tiles = -(-used // 1024)
    flat = jnp.pad(flat, (0, tiles * 1024 - used)).reshape(tiles * 8, 128)
    tables = gather_indices(flat, n_reg, n).reshape(n, n_reg, tiles * 1024)
    all_slots = jnp.swapaxes(tables[:, :, :seg_local], 0, 1).reshape(-1)
    lists = lax.dynamic_index_in_dim(tables, reg, axis=1, keepdims=False)
    lists = lists[:, seg_local:used].reshape(n, blocks, overlap)
    numbers = jnp.arange(all_slots.shape[0], dtype=jnp.int32)
    wanted = jnp.sum(jnp.where(lists[..., None] == numbers, all_slots, 0), axis=-1)
    wanted = wanted - reg * (n * seg_local)
    mine = wanted // seg_local == me
    pick = jnp.sum(jnp.where(mine, wanted % seg_local, 0), axis=-1)
    steps = stride_for(n) * jnp.arange(n, dtype=jnp.int32)
    targets = (me + steps) % n
    chosen = targets[:, None, None] == jnp.arange(n, dtype=jnp.int32)[None, :, None]
    pick = jnp.sum(jnp.where(chosen, pick[None], 0), axis=1)
    all_live = overlap == n
    if all_live:
        live = pick
    else:
        own = lax.dynamic_index_in_dim(wanted, me, axis=0, keepdims=False) // seg_local
        sources = (me - steps) % n
        live = jnp.any(own[None] == sources[:, None, None], axis=-1).astype(jnp.int32)

    weights = (query_weight, key_weight, value_weight, mixer_weight, packed_weight)
    mixed, returned = both_attentions(
        pick, live, scan_tokens.reshape(seg_local, SEG, model_width), grid_tokens, weights,
        n, blocks, all_live,
    )
    return (
        mixed.astype(jnp.float32)
        + jnp.dot(returned, merged_weight, preferred_element_type=jnp.float32)
    ).astype(jnp.bfloat16)


def solution(mesh):
    in_specs = (
        P(("region", "seq"), None),
        P(("region", "seq"), None),
        P(("region", "seq")),
        P(("region", "seq"), None),
        P(),
        P(),
        P(),
        P(),
        P(),
        P(),
    )
    out_specs = P(("region", "seq"), None)
    return jax.shard_map(
        on_device, mesh=mesh, in_specs=in_specs, out_specs=out_specs, check_vma=False
    )
```
